128 devices in a mesh: dp: 8 (over z_hi, y), tp: 16 (over x, z_lo, core).
Axes of the slice: x: 4, y: 4, z: 4 (z_hi: 2, z_lo: 2; z = z_hi * 2 + z_lo), core: 2. Of those that a mesh axis runs over, the one named last changes fastest.
Arguments:
- residual: bfloat16 [2, 1024, 7168], P(None, ('dp', 'tp')), may hold values from -3 to 3
- queries: bfloat16 [2, 1024, 64, 576], P(None, ('dp', 'tp')), may hold values from -28 to 28
- latent_cache: bfloat16 [2, 1024, 256, 576], P(None, ('dp', 'tp')), may hold values from -6 to 6
- new_latent: bfloat16 [2, 1024, 576], P(None, ('dp', 'tp')), may hold values from -6 to 6
- lengths: int32 [2, 1024], P(None, ('dp', 'tp')), may hold values from 1 to 256, as said below
- positions: int32 [2, 1024], P(None, ('dp', 'tp')), may hold values from 0 to 8191
- latent_value_weight: bfloat16 [64, 512, 128], P('tp'), may hold values from -3 to 3
- w_out: bfloat16 [8192, 7168], P('tp'), may hold values from -0.0625 to 0.0625
- norm_gain: bfloat16 [7168], replicated, may hold values from 0.099609375 to 1.8984375
- gate_weight: bfloat16 [7168, 10240], P(None, 'tp'), may hold values from -0.0625 to 0.0625
- up_weight: bfloat16 [7168, 10240], P(None, 'tp'), may hold values from -0.0625 to 0.0625
Outputs:
- after_attention: bfloat16 [2, 1024, 7168], P(None, ('dp', 'tp'))
- activation: bfloat16 [2, 1024, 10240], P(None, 'dp', 'tp')
The draws below stay inside these ranges and needn't reach their ends.
Inputs may be any that keep to these rules, and one draw needn't show every extreme that they name: `lengths`: in each micro-batch one row holds exactly 256 cached tokens and another exactly 1.
All inputs are finite; a program needn't handle non-finite values.
Results may differ from the reference program's by a relative error of at most 0.039.
Values may be sent and summed in bfloat16 or wider, within the bound.
No kernel may reach another device: no remote copies, remote signals or barrier semaphores. Data moves between devices by JAX's collectives and lax.ppermute only.
A program may use at most 128 MiB of HBM per device.

```python
import jax
import jax.numpy as jnp
from jax import lax

D = 7168
H = 64
LATENT = 512
ROPE = 64
VDIM = 128
FF = 10240
MAXLEN = 256
MICRO = 2
ROWS = 1024


def draw_queries(key, part):
    key = jax.random.fold_in(key, 1)
    drawn = jnp.clip(jax.random.normal(key, (MICRO, ROWS, H, LATENT + ROPE), jnp.float32), -6.0, 6.0)
    return drawn.astype(jnp.bfloat16)


def draw_latent_cache(key, part):
    key = jax.random.fold_in(key, 2)
    drawn = jnp.clip(jax.random.normal(key, (MICRO, ROWS, MAXLEN, LATENT + ROPE), jnp.float32), -6.0, 6.0)
    return drawn.astype(jnp.bfloat16)


def draw_new_latent(key, part):
    key = jax.random.fold_in(key, 3)
    drawn = jnp.clip(jax.random.normal(key, (MICRO, ROWS, LATENT + ROPE), jnp.float32), -6.0, 6.0)
    return drawn.astype(jnp.bfloat16)


def draw_lengths(key, part):
    key = jax.random.fold_in(key, 5)
    first_key, second_key, pick_key = jax.random.split(key, 3)
    first_draw = jax.random.randint(first_key, (MICRO, ROWS), 0, MAXLEN)
    second_draw = jax.random.randint(second_key, (MICRO, ROWS), 0, MAXLEN)
    drawn = MAXLEN - first_draw * second_draw // MAXLEN
    longest = jax.random.randint(pick_key, (MICRO, 1), 0, ROWS)
    shortest = (longest + 1) % ROWS
    row_ids = jnp.arange(ROWS)[None, :]
    drawn = jnp.where(row_ids == longest, MAXLEN, drawn)
    drawn = jnp.where(row_ids == shortest, 1, drawn)
    return drawn.astype(jnp.int32)


def with_ends(values, key, least, high):
    longest = values.shape.index(max(values.shape))
    spots = []
    for shift in (0, 1):
        where = [jax.random.randint(jax.random.fold_in(key, axis), (), 0, length) for axis, length in enumerate(values.shape)]
        where[longest] = (where[longest] + shift) % values.shape[longest]
        spots.append(tuple(where))
    return values.at[spots[0]].set(least).at[spots[1]].set(high)


def block_levels(rng, extent, cuts, low, largest):
    def one(axis_at, blocks):
        draws = jax.random.uniform(jax.random.fold_in(jax.random.fold_in(rng, 6), axis_at), (blocks,), jnp.float32, low / len(cuts), largest / len(cuts))
        return jnp.repeat(jnp.exp(draws), extent[axis_at] // blocks).reshape((-1,) + (1,) * (len(extent) - axis_at - 1))

    level = one(*cuts[0])
    for cut in cuts[1:]:
        level = level * one(*cut)
    return level


def scatter_about(own_key, shape, deviation, most, shards=(), kind=jnp.bfloat16):
    result = jax.random.normal(own_key, shape, jnp.float32) * deviation
    if len(shards) > 0:
        result = block_levels(own_key, shape, shards, -0.22, 0.18) * result
    return jnp.clip(result, min=-most, max=most).astype(kind)


def setup_inputs(seed: int = 0) -> dict:
    seeds = jax.random.split(jax.random.key(seed), 12)
    residual = scatter_about(seeds[0], (MICRO, ROWS, D), 0.5, 3.0, ((1, 128),))
    queries = draw_queries(jax.random.fold_in(seeds[11], 71), 0)
    latent_cache = draw_latent_cache(jax.random.fold_in(seeds[11], 71), 0)
    new_latent = draw_new_latent(jax.random.fold_in(seeds[11], 71), 0)
    lengths = draw_lengths(jax.random.fold_in(seeds[11], 71), 0)
    positions = with_ends(jax.random.randint(seeds[5], (MICRO, ROWS), 0, 8192), jax.random.fold_in(seeds[5], 1), 0, 8191).astype(jnp.int32)
    latent_value_weight = scatter_about(seeds[6], (H, LATENT, VDIM), 4 ** -0.5, 3.0, ((0, 16),))
    w_out = scatter_about(seeds[7], (H * VDIM, D), (H * VDIM) ** -0.5, 0.0625, ((0, 16),))
    norm_gain = jnp.clip(1.0 + 0.18 * jax.random.normal(seeds[8], (D,), jnp.float32), 0.099609375, 1.8984375).astype(jnp.bfloat16)
    gate_weight = scatter_about(seeds[9], (D, FF), D ** -0.5, 0.0625, ((1, 16),))
    up_weight = scatter_about(seeds[10], (D, FF), D ** -0.5, 0.0625, ((1, 16),))
    return dict(residual=residual, queries=queries, latent_cache=latent_cache, new_latent=new_latent, lengths=lengths, positions=positions, latent_value_weight=latent_value_weight, w_out=w_out, norm_gain=norm_gain, gate_weight=gate_weight, up_weight=up_weight)


score_scale = 192.0 ** (-0.5)

def rotary(values, position):
    half_width = values.shape[-1] // 2
    exponent = jnp.arange(half_width, dtype=jnp.float32) * (2.0 / values.shape[-1])
    frequency = 10000.0 ** (-exponent)
    angles = position.astype(jnp.float32)[..., None] * frequency
    cosine = jnp.cos(angles)
    sine_part = jnp.sin(angles)
    leading = values[..., :half_width]
    trailing = values[..., half_width:]
    return jnp.concatenate([leading * cosine - trailing * sine_part, leading * sine_part + trailing * cosine], axis=-1)

def reference(residual, queries, latent_cache, new_latent, lengths, positions, latent_value_weight, w_out, norm_gain, gate_weight, up_weight):
    query_rope = rotary(queries[..., LATENT:].astype(jnp.float32), positions[..., None]).astype(jnp.bfloat16)
    query_all = jnp.concatenate([queries[..., :LATENT], query_rope], axis=-1)
    key_rope = rotary(new_latent[..., LATENT:].astype(jnp.float32), positions).astype(jnp.bfloat16)
    new_key = jnp.concatenate([new_latent[..., :LATENT], key_rope], axis=-1)
    slots = jnp.arange(MAXLEN + 1).astype(jnp.int32)

    def one_row(packed):
        query_row, cache_row, new_row, length_row = packed
        key_rows = jnp.concatenate([cache_row, new_row[None, :]], axis=0)
        scores = jnp.dot(query_row, jnp.transpose(key_rows), preferred_element_type=jnp.float32) * score_scale
        visible = (slots < length_row) | (slots == MAXLEN)
        scores = jnp.where(visible[None, :], scores, -1e+30)
        peak_score = lax.optimization_barrier(jnp.max(scores, axis=-1, keepdims=True))
        weights = jnp.where(visible[None, :], jnp.exp(scores - peak_score), 0.0)
        totals = lax.optimization_barrier(jnp.sum(weights, axis=-1, keepdims=True))
        context = jnp.dot(weights.astype(jnp.bfloat16), key_rows[:, :LATENT], preferred_element_type=jnp.float32)
        return (context / totals).astype(jnp.bfloat16)
    attended_latent = lax.map(one_row, (query_all.reshape(-1, H, LATENT + ROPE), latent_cache.reshape(-1, MAXLEN, LATENT + ROPE), new_key.reshape(-1, LATENT + ROPE), lengths.reshape(-1)))
    attended_latent = attended_latent.reshape(MICRO, ROWS, H, LATENT).astype(jnp.float32)
    value_matrix_rows = jnp.einsum('sqwy,wyd->sqwd', attended_latent, latent_value_weight.astype(jnp.float32)).astype(jnp.bfloat16)
    flat_value = value_matrix_rows.reshape(MICRO * ROWS, H * VDIM)
    attention_out = jnp.dot(flat_value, w_out, preferred_element_type=jnp.float32).reshape(MICRO, ROWS, D)
    after_attention = (residual.astype(jnp.float32) + attention_out).astype(jnp.bfloat16)
    widened = after_attention.astype(jnp.float32)
    mean_square = lax.optimization_barrier(jnp.mean(widened * widened, axis=-1, keepdims=True))
    normed = (widened * lax.rsqrt(mean_square + 1e-06) * norm_gain.astype(jnp.float32)).astype(jnp.bfloat16)
    flat_normed = normed.reshape(MICRO * ROWS, D)
    gate_activation = jnp.dot(flat_normed, gate_weight, preferred_element_type=jnp.float32)
    up_projected = jnp.dot(flat_normed, up_weight, preferred_element_type=jnp.float32)
    activation = (jax.nn.silu(gate_activation) * up_projected).astype(jnp.bfloat16).reshape(MICRO, ROWS, FF)
    return (after_attention, activation)
```

```python
import functools

import jax
import jax.numpy as jnp
import numpy as np
from jax import lax
from jax.experimental import pallas as pl
from jax.experimental.pallas import tpu as pltpu
from jax.sharding import PartitionSpec as P

score_scale = 192.0 ** (-0.5)
neg_large = -1e30
f32 = jnp.float32
bf16 = jnp.bfloat16
vmem_limit = 48 * 1024 * 1024
x_size, z_size, core_size = 4, 2, 2
tp_size = x_size * z_size * core_size


def tp_perm(dx=0, dz=0, dc=0):
    pairs = []
    for i in range(tp_size):
        x, z, c = i // 4, (i // 2) % 2, i % 2
        pairs.append((i, ((x + dx) % 4) * 4 + (z ^ dz) * 2 + (c ^ dc)))
    return pairs


def send(value, dx=0, dz=0, dc=0):
    return lax.ppermute(value, "tp", tp_perm(dx, dz, dc))


def rotary_tables(positions, rope):
    half = rope // 2
    exponent = jnp.arange(half, dtype=f32) * (2.0 / rope)
    angles = positions.astype(f32)[..., None] * (10000.0 ** (-exponent))
    cosine, sine = jnp.cos(angles), jnp.sin(angles)
    return jnp.concatenate([cosine, cosine, -sine, sine], axis=-1)


def attention_kernel(rows, latent, len_ref, q_ref, c_ref, n_ref, t_ref, out_ref, held):
    step = pl.program_id(0)
    rope = q_ref.shape[-1] - latent
    slots = c_ref.shape[1]
    half = rope // 2

    def turn(values, cosine, sine):
        swapped = jnp.concatenate([values[:, half:], values[:, :half]], axis=-1)
        return (values * cosine + swapped * sine).astype(bf16)

    for r in range(rows):
        row = step * rows + r
        length = len_ref[row]
        table = t_ref[r : r + 1, :]
        cosine, sine = table[:, :rope], table[:, rope:]
        q_lat = q_ref[r, :, :latent]
        q_rope = turn(q_ref[r, :, latent:].astype(f32), cosine, sine)
        n_lat = n_ref[r : r + 1, :latent].astype(f32)
        n_rope = turn(n_ref[r : r + 1, latent:].astype(f32), cosine, sine).astype(f32)
        dims = (((1,), (1,)), ((), ()))
        scores = lax.dot_general(q_lat, c_ref[r, :, :latent], dims, preferred_element_type=f32)
        scores += lax.dot_general(q_rope, c_ref[r, :, latent:], dims, preferred_element_type=f32)
        own = jnp.sum(q_lat.astype(f32) * n_lat, axis=-1, keepdims=True)
        own += jnp.sum(q_rope.astype(f32) * n_rope, axis=-1, keepdims=True)
        own = own * score_scale
        visible = lax.broadcasted_iota(jnp.int32, scores.shape, 1) < length
        scores = jnp.where(visible, scores * score_scale, neg_large)
        top = jnp.maximum(jnp.max(scores, axis=-1, keepdims=True), own)
        weights = jnp.where(visible, jnp.exp(scores - top), 0.0)
        own_weight = jnp.exp(own - top)
        total = jnp.sum(weights, axis=-1, keepdims=True) + own_weight
        context = jnp.dot(weights.astype(bf16), c_ref[r, :, :latent], preferred_element_type=f32)
        context += own_weight.astype(bf16).astype(f32) * n_lat
        held[:, row, :] = context * (1.0 / total)

    @pl.when(step == pl.num_programs(0) - 1)
    def _():
        out_ref[...] = held[...].astype(bf16)


def attention(queries, cache, new_latent, lengths, tables, latent):
    count, heads, width = queries.shape
    slots = cache.shape[1]
    rows = 8
    return pl.pallas_call(
        functools.partial(attention_kernel, rows, latent),
        grid_spec=pltpu.PrefetchScalarGridSpec(
            num_scalar_prefetch=1,
            grid=(count // rows,),
            in_specs=[
                pl.BlockSpec((rows, heads, width), lambda i, n: (i, 0, 0)),
                pl.BlockSpec((rows, slots, width), lambda i, n: (i, 0, 0)),
                pl.BlockSpec((rows, width), lambda i, n: (i, 0)),
                pl.BlockSpec((rows, tables.shape[1]), lambda i, n: (i, 0)),
            ],
            out_specs=pl.BlockSpec((heads, count, latent), lambda i, n: (0, 0, 0)),
            scratch_shapes=[pltpu.VMEM((heads, count, latent), f32)],
        ),
        out_shape=jax.ShapeDtypeStruct((heads, count, latent), bf16),
        compiler_params=pltpu.CompilerParams(vmem_limit_bytes=vmem_limit),
        cost_estimate=pl.CostEstimate(
            flops=4 * count * heads * width * slots,
            bytes_accessed=2 * count * width * (heads + slots),
            transcendentals=count * heads * slots,
        ),
        name="attention",
    )(lengths, queries, cache, new_latent, tables)


def value_kernel(block, order_ref, a_ref, v_ref, w_ref, send_ref, keep_ref, value_ref, gathered):
    step = pl.program_id(0)
    heads, width = v_ref.shape[0], v_ref.shape[2]

    @pl.when(step == 0)
    def _():
        for p in range(tp_size):
            gathered[:, p * block : (p + 1) * block, :] = a_ref[order_ref[p]]
        for h in range(heads):
            value_ref[:, h * width : (h + 1) * width] = jnp.dot(
                gathered[h], v_ref[h], preferred_element_type=f32
            ).astype(bf16)

    project(value_ref[...], w_ref, send_ref, keep_ref, block, True)


def project(values, w_ref, send_ref, keep_ref, block, x_major):
    half = values.shape[0] // 2
    if x_major:
        parts = []
        for c in range(core_size):
            for px in range(x_size):
                for pz in range(z_size):
                    at = ((c * z_size + pz) * x_size + px) * block
                    parts.append(values[at : at + block])
        values = jnp.concatenate(parts, axis=0)
    result = jnp.dot(values, w_ref[...], preferred_element_type=f32).astype(bf16)
    keep_ref[...] = result[:half]
    send_ref[...] = result[half:]


def out_kernel(block, v_ref, w_ref, send_ref, keep_ref):
    project(v_ref[...], w_ref, send_ref, keep_ref, block, False)


def value_and_out(order, arrived, value_weight, w_out, columns, tile):
    sources, heads, block, latent = arrived.shape
    rows = sources * block
    depth = w_out.shape[0]
    return pl.pallas_call(
        functools.partial(value_kernel, block),
        grid_spec=pltpu.PrefetchScalarGridSpec(
            num_scalar_prefetch=1,
            grid=(columns // tile,),
            in_specs=[
                pl.BlockSpec(arrived.shape, lambda i, o: (0, 0, 0, 0)),
                pl.BlockSpec(value_weight.shape, lambda i, o: (0, 0, 0)),
                pl.BlockSpec((depth, tile), lambda i, o: (0, i)),
            ],
            out_specs=[
                pl.BlockSpec((rows // 2, tile), lambda i, o: (0, i)),
                pl.BlockSpec((rows // 2, tile), lambda i, o: (0, i)),
                pl.BlockSpec((rows, depth), lambda i, o: (0, 0)),
            ],
            scratch_shapes=[pltpu.VMEM((heads, rows, latent), bf16)],
        ),
        out_shape=[
            jax.ShapeDtypeStruct((rows // 2, columns), bf16),
            jax.ShapeDtypeStruct((rows // 2, columns), bf16),
            jax.ShapeDtypeStruct((rows, depth), bf16),
        ],
        compiler_params=pltpu.CompilerParams(vmem_limit_bytes=vmem_limit),
        cost_estimate=pl.CostEstimate(
            flops=2 * rows * depth * (columns + latent),
            bytes_accessed=2 * depth * columns,
            transcendentals=0,
        ),
        name="value_out",
    )(order, arrived, value_weight, w_out)


def out_only(values, w_out, block, start, columns, tile):
    rows, depth = values.shape
    first = start // tile
    return pl.pallas_call(
        functools.partial(out_kernel, block),
        grid=(columns // tile,),
        in_specs=[
            pl.BlockSpec((rows, depth), lambda i: (0, 0)),
            pl.BlockSpec((depth, tile), lambda i: (0, first + i)),
        ],
        out_specs=[
            pl.BlockSpec((rows // 2, tile), lambda i: (0, i)),
            pl.BlockSpec((rows // 2, tile), lambda i: (0, i)),
        ],
        out_shape=[
            jax.ShapeDtypeStruct((rows // 2, columns), bf16),
            jax.ShapeDtypeStruct((rows // 2, columns), bf16),
        ],
        compiler_params=pltpu.CompilerParams(vmem_limit_bytes=vmem_limit),
        cost_estimate=pl.CostEstimate(
            flops=2 * rows * depth * columns, bytes_accessed=2 * depth * columns, transcendentals=0
        ),
        name="out_proj",
    )(values, w_out)


def gated_kernel(layout, first, last, width, *refs):
    pieces = 1 + max(p for p, _ in layout)
    refs = list(refs)
    order_ref = refs.pop(0)
    x_refs = [refs.pop(0) for _ in range(pieces)]
    gain_ref, gate_ref, up_ref = refs.pop(0), refs.pop(0), refs.pop(0)
    if not first:
        acc_in, square_in = refs.pop(0), refs.pop(0)
    if last:
        out_ref, acc_ref, square_ref, ordered = refs
    else:
        acc_ref, square_ref = refs
    step = pl.program_id(0)
    block = 16

    @pl.when(step == 0)
    def _():
        if first:
            acc_ref[...] = jnp.zeros_like(acc_ref)
            square_ref[...] = jnp.zeros_like(square_ref)
        else:
            acc_ref[...] = acc_in[...]
            square_ref[...] = square_in[...]

    wide = jnp.concatenate([x_refs[p][at : at + block] for p, at in layout], axis=0).astype(f32)
    squares = wide * wide
    lanes = square_ref.shape[1]
    total = square_ref[...]
    for k in range(0, wide.shape[1], lanes):
        total += squares[:, k : k + lanes]
    square_ref[...] = total
    scaled = (wide * gain_ref[...].astype(f32)).astype(bf16)
    weights = jnp.concatenate([gate_ref[...], up_ref[...]], axis=1)
    acc_ref[...] += jnp.dot(scaled, weights, preferred_element_type=f32)

    if last:

        @pl.when(step == pl.num_programs(0) - 1)
        def _():
            hidden = out_ref.shape[2]
            mean = jnp.sum(square_ref[...], axis=-1, keepdims=True) * (1.0 / width)
            scale = lax.rsqrt(mean + 1e-06)
            gate = acc_ref[:, :hidden] * scale
            up = acc_ref[:, hidden:] * scale
            active = gate / (1.0 + jnp.exp(-gate)) * up
            for p in range(tp_size):
                at = pl.multiple_of(order_ref[p] * 8, 8)
                for m in range(2):
                    begin = p * block + m * 8
                    ordered[m, pl.ds(at, 8), :] = active[begin : begin + 8]
            out_ref[...] = ordered[...].astype(bf16)


def gated(order, pieces, layout, gain, gate, up, start, tile, carried, width):
    first = carried is None
    last = not first
    columns = pieces[0].shape[1]
    hidden = gate.shape[1]
    rows = sum(p.shape[0] for p in pieces)
    base = start // tile
    in_specs = [pl.BlockSpec((p.shape[0], tile), lambda i, o: (0, i)) for p in pieces]
    in_specs += [
        pl.BlockSpec((1, tile), lambda i, o: (0, base + i)),
        pl.BlockSpec((tile, hidden), lambda i, o: (base + i, 0)),
        pl.BlockSpec((tile, hidden), lambda i, o: (base + i, 0)),
    ]
    args = list(pieces) + [gain, gate, up]
    acc_shape, square_shape = (rows, 2 * hidden), (rows, 128)
    whole = lambda i, o: (0, 0)
    if not first:
        in_specs += [pl.BlockSpec(acc_shape, whole), pl.BlockSpec(square_shape, whole)]
        args += list(carried)
    if last:
        out_dims = (2, rows // 2, hidden)
        out_specs = pl.BlockSpec(out_dims, lambda i, o: (0, 0, 0))
        out_shape = jax.ShapeDtypeStruct(out_dims, bf16)
        scratch = [
            pltpu.VMEM(acc_shape, f32),
            pltpu.VMEM(square_shape, f32),
            pltpu.VMEM(out_dims, f32),
        ]
    else:
        out_specs = [pl.BlockSpec(acc_shape, whole), pl.BlockSpec(square_shape, whole)]
        out_shape = [jax.ShapeDtypeStruct(acc_shape, f32), jax.ShapeDtypeStruct(square_shape, f32)]
        scratch = []
    return pl.pallas_call(
        functools.partial(gated_kernel, layout, first, last, width),
        grid_spec=pltpu.PrefetchScalarGridSpec(
            num_scalar_prefetch=1,
            grid=(columns // tile,),
            in_specs=in_specs,
            out_specs=out_specs,
            scratch_shapes=scratch,
        ),
        out_shape=out_shape,
        compiler_params=pltpu.CompilerParams(vmem_limit_bytes=vmem_limit),
        cost_estimate=pl.CostEstimate(
            flops=4 * rows * columns * hidden,
            bytes_accessed=4 * columns * hidden,
            transcendentals=0,
        ),
        name="gated_pair",
    )(order, *args)


def shards(
    residual,
    queries,
    latent_cache,
    new_latent,
    lengths,
    positions,
    latent_value_weight,
    w_out,
    norm_gain,
    gate_weight,
    up_weight,
):
    latent = latent_value_weight.shape[1]
    micro, own_rows, width = residual.shape
    block = micro * own_rows
    heads = queries.shape[2]
    me = lax.axis_index("tp")
    my_x, my_z, my_c = me // 4, (me // 2) % 2, me % 2
    order = jnp.stack(
        [
            ((my_x + px) % 4) * 4 + (my_z ^ pz) * 2 + (my_c ^ pc)
            for pc in range(core_size)
            for pz in range(z_size)
            for px in range(x_size)
        ]
    ).astype(jnp.int32)
    tables = rotary_tables(positions.reshape(-1), queries.shape[3] - latent)
    attended = attention(
        queries.reshape((block,) + queries.shape[2:]),
        latent_cache.reshape((block,) + latent_cache.shape[2:]),
        new_latent.reshape(block, -1),
        lengths.reshape(-1),
        tables,
        latent,
    )
    arrived = lax.all_to_all(
        attended.reshape(tp_size, heads // tp_size, block, latent),
        "tp",
        split_axis=0,
        concat_axis=0,
        tiled=True,
    )
    tile = 1792
    cut = 3584
    send_a, keep_a, values = value_and_out(order, arrived, latent_value_weight, w_out, cut, tile)
    send_b, keep_b = out_only(values, w_out, block, cut, width - cut, tile)
    flat_residual = residual.reshape(block, width).astype(f32)

    def add(*parts):
        total = parts[0].astype(f32)
        for part in parts[1:]:
            total = total + part.astype(f32)
        return total

    def x_sum(value, rows):
        own = value[:rows]
        right = send(value[rows : 2 * rows], dx=1)
        left = send(value[3 * rows : 4 * rows], dx=3)
        across = send(value[2 * rows : 3 * rows], dx=2)
        return own, right, left, across

    pair_a = add(keep_a, send(send_a, dc=1)).astype(bf16)
    pair_b = add(keep_b, send(send_b, dc=1)).astype(bf16)
    line_a = add(*x_sum(pair_a, 2 * block)).astype(bf16)
    line_b = add(pair_b[: 4 * block], send(pair_b[4 * block :], dz=1)).astype(bf16)
    after_a = add(
        flat_residual[:, :cut], line_a[:block], send(line_a[block:], dz=1)
    ).astype(bf16)
    after_b = add(flat_residual[:, cut:], *x_sum(line_b, block)).astype(bf16)

    def x_gather(value):
        return [value, send(value, dx=3), send(value, dx=2), send(value, dx=1)]

    near_a = jnp.concatenate(x_gather(after_a), axis=0)
    far_a = send(near_a, dz=1)
    pieces_a = [near_a, far_a, send(near_a, dc=1), send(far_a, dc=1)]
    both_b = jnp.concatenate([after_b, send(after_b, dz=1)], axis=0)
    gathered_b = x_gather(both_b)
    pieces_b = gathered_b + [send(g, dc=1) for g in gathered_b]

    canonical = [
        (pc, pz, px) for pc in range(core_size) for pz in range(z_size) for px in range(x_size)
    ]
    layout_a = [(pc * 2 + pz, px * block) for pc, pz, px in canonical]
    layout_b = [(pc * 4 + px, pz * block) for pc, pz, px in canonical]
    gain_row = norm_gain.reshape(1, width)
    k_tile = 512
    carried = gated(
        order, pieces_a, layout_a, gain_row, gate_weight, up_weight, 0, k_tile, None, width
    )
    activation = gated(
        order, pieces_b, layout_b, gain_row, gate_weight, up_weight, cut, k_tile, carried, width
    )
    after_attention = jnp.concatenate([after_a, after_b], axis=1).reshape(residual.shape)
    return (after_attention, activation)


def solution(mesh):
    return jax.shard_map(
        shards,
        mesh=mesh,
        in_specs=(
            P(None, ("dp", "tp"), None),
            P(None, ("dp", "tp"), None, None),
            P(None, ("dp", "tp"), None, None),
            P(None, ("dp", "tp"), None),
            P(None, ("dp", "tp")),
            P(None, ("dp", "tp")),
            P("tp", None, None),
            P("tp", None),
            P(),
            P(None, "tp"),
            P(None, "tp"),
        ),
        out_specs=(P(None, ("dp", "tp"), None), P(None, "dp", "tp")),
        check_vma=False,
    )
```

```python
import functools

import jax
import jax.numpy as jnp
import numpy as np
from jax import lax
from jax.experimental import pallas as pl
from jax.experimental.pallas import tpu as pltpu
from jax.sharding import PartitionSpec as P

score_scale = 192.0 ** (-0.5)
neg_large = -1e30
f32 = jnp.float32
bf16 = jnp.bfloat16
vmem_limit = 20 * 1024 * 1024
large_vmem = 56 * 1024 * 1024
x_size, z_size, core_size = 4, 2, 2
tp_size = x_size * z_size * core_size


def tp_perm(dx=0, dz=0, dc=0):
    pairs = []
    for i in range(tp_size):
        x, z, c = i // 4, (i // 2) % 2, i % 2
        pairs.append((i, ((x + dx) % 4) * 4 + (z ^ dz) * 2 + (c ^ dc)))
    return pairs


def send(value, dx=0, dz=0, dc=0):
    return lax.ppermute(value, "tp", tp_perm(dx, dz, dc))


def rotary_tables(positions, rope):
    half = rope // 2
    exponent = jnp.arange(half, dtype=f32) * (2.0 / rope)
    angles = positions.astype(f32)[..., None] * (10000.0 ** (-exponent))
    cosine, sine = jnp.cos(angles), jnp.sin(angles)
    return jnp.concatenate([cosine, cosine, -sine, sine], axis=-1)


def attention_kernel(
    group, span, latent, len_ref, q_hbm, c_hbm, n_ref, t_ref, out_ref, q_ref, c_ref, held, q_sem, c_sem
):
    count, heads, width = q_ref.shape
    rope = width - latent
    half = rope // 2
    per = len_ref.shape[1]

    copies = []
    for i in range(count // span):
        at = pl.ds(i * span, span)
        copies.append(
            (
                pltpu.make_async_copy(q_hbm.at[at], q_ref.at[at], q_sem.at[i]),
                pltpu.make_async_copy(c_hbm.at[at], c_ref.at[at], c_sem.at[i]),
            )
        )
    for pair in copies:
        for copy in pair:
            copy.start()

    def turn(values, cosine, sine):
        swapped = jnp.concatenate([values[:, half:], values[:, :half]], axis=-1)
        return (values * cosine + swapped * sine).astype(bf16)

    for begin in range(0, count, group):
        scored = []
        for r in range(begin, begin + group):
            if r % span == 0:
                for copy in copies[r // span]:
                    copy.wait()
            table = t_ref[r : r + 1, :]
            cosine, sine = table[:, :rope], table[:, rope:]
            q_lat = q_ref[r, :, :latent]
            q_rope = turn(q_ref[r, :, latent:].astype(f32), cosine, sine)
            n_lat = n_ref[r : r + 1, :latent].astype(f32)
            n_rope = turn(n_ref[r : r + 1, latent:].astype(f32), cosine, sine).astype(f32)
            scores = jnp.dot(q_lat, c_ref[r, :latent, :], preferred_element_type=f32)
            scores += jnp.dot(q_rope, c_ref[r, latent:, :], preferred_element_type=f32)
            own = jnp.sum(q_lat.astype(f32) * n_lat, axis=-1, keepdims=True)
            own += jnp.sum(q_rope.astype(f32) * n_rope, axis=-1, keepdims=True)
            scored.append((scores, own * score_scale, n_lat))
        weighted = []
        for r in range(begin, begin + group):
            scores, own, n_lat = scored[r - begin]
            visible = lax.broadcasted_iota(jnp.int32, scores.shape, 1) < len_ref[r // per, r % per]
            scores = jnp.where(visible, scores * score_scale, neg_large)
            top = jnp.maximum(jnp.max(scores, axis=-1, keepdims=True), own)
            weights = jnp.where(visible, jnp.exp(scores - top), 0.0)
            own_weight = jnp.exp(own - top)
            total = jnp.sum(weights, axis=-1, keepdims=True) + own_weight
            weighted.append((weights.astype(bf16), own_weight, total, n_lat))
        for r in range(begin, begin + group):
            weights, own_weight, total, n_lat = weighted[r - begin]
            context = lax.dot_general(
                weights, c_ref[r, :latent, :], (((1,), (1,)), ((), ())), preferred_element_type=f32
            )
            context += own_weight.astype(bf16).astype(f32) * n_lat
            held[:, r, :] = context * (1.0 / total)
    out_ref[...] = held[...].astype(bf16)


def attention(queries, cache, new_latent, lengths, tables, latent, group=8, span=8):
    count, heads, width = queries.shape
    slots = cache.shape[2]
    vmem = pl.BlockSpec(memory_space=pltpu.VMEM)
    return pl.pallas_call(
        functools.partial(attention_kernel, group, span, latent),
        in_specs=[
            pl.BlockSpec(memory_space=pltpu.SMEM),
            pl.BlockSpec(memory_space=pltpu.HBM),
            pl.BlockSpec(memory_space=pltpu.HBM),
            vmem,
            vmem,
        ],
        out_specs=vmem,
        scratch_shapes=[
            pltpu.VMEM(queries.shape, bf16),
            pltpu.VMEM(cache.shape, bf16),
            pltpu.VMEM((heads, count, latent), f32),
            pltpu.SemaphoreType.DMA((count // span,)),
            pltpu.SemaphoreType.DMA((count // span,)),
        ],
        out_shape=jax.ShapeDtypeStruct((heads, count, latent), bf16),
        compiler_params=pltpu.CompilerParams(vmem_limit_bytes=vmem_limit),
        cost_estimate=pl.CostEstimate(
            flops=4 * count * heads * width * slots,
            bytes_accessed=2 * count * width * (heads + slots),
            transcendentals=count * heads * slots,
        ),
        name="attention",
    )(lengths, queries, cache, new_latent, tables)


def value_kernel(block, order_ref, a_ref, v_ref, w_ref, send_ref, keep_ref, value_ref, gathered):
    step = pl.program_id(0)
    heads, width = v_ref.shape[0], v_ref.shape[2]

    @pl.when(step == 0)
    def _():
        for p in range(tp_size):
            gathered[:, p * block : (p + 1) * block, :] = a_ref[order_ref[p]]
        for h in range(heads):
            value_ref[:, h * width : (h + 1) * width] = jnp.dot(
                gathered[h], v_ref[h], preferred_element_type=f32
            ).astype(bf16)

    project(value_ref[...], w_ref, send_ref, keep_ref, block, False)


def project(values, w_ref, send_ref, keep_ref, block, x_major):
    half = values.shape[0] // 2
    if x_major:
        parts = []
        for c in range(core_size):
            for px in range(x_size):
                for pz in range(z_size):
                    at = ((c * z_size + pz) * x_size + px) * block
                    parts.append(values[at : at + block])
        values = jnp.concatenate(parts, axis=0)
    result = jnp.dot(values, w_ref[...], preferred_element_type=f32).astype(bf16)
    keep_ref[...] = result[:half]
    send_ref[...] = result[half:]


def out_kernel(block, v_ref, w_ref, send_ref, keep_ref):
    project(v_ref[...], w_ref, send_ref, keep_ref, block, True)


def value_and_out(order, arrived, value_weight, w_out, start, columns, tile):
    sources, heads, block, latent = arrived.shape
    rows = sources * block
    depth = w_out.shape[0]
    first = start // tile
    return pl.pallas_call(
        functools.partial(value_kernel, block),
        grid_spec=pltpu.PrefetchScalarGridSpec(
            num_scalar_prefetch=1,
            grid=(columns // tile,),
            in_specs=[
                pl.BlockSpec(arrived.shape, lambda i, o: (0, 0, 0, 0)),
                pl.BlockSpec(value_weight.shape, lambda i, o: (0, 0, 0)),
                pl.BlockSpec((depth, tile), lambda i, o: (0, first + i)),
            ],
            out_specs=[
                pl.BlockSpec((rows // 2, tile), lambda i, o: (0, i)),
                pl.BlockSpec((rows // 2, tile), lambda i, o: (0, i)),
                pl.BlockSpec((rows, depth), lambda i, o: (0, 0)),
            ],
            scratch_shapes=[pltpu.VMEM((heads, rows, latent), bf16)],
        ),
        out_shape=[
            jax.ShapeDtypeStruct((rows // 2, columns), bf16),
            jax.ShapeDtypeStruct((rows // 2, columns), bf16),
            jax.ShapeDtypeStruct((rows, depth), bf16),
        ],
        compiler_params=pltpu.CompilerParams(vmem_limit_bytes=large_vmem),
        cost_estimate=pl.CostEstimate(
            flops=2 * rows * depth * (columns + latent),
            bytes_accessed=2 * depth * columns,
            transcendentals=0,
        ),
        name="value_out",
    )(order, arrived, value_weight, w_out)


def out_only(values, w_out, block, start, columns, tile):
    rows, depth = values.shape
    first = start // tile
    return pl.pallas_call(
        functools.partial(out_kernel, block),
        grid=(columns // tile,),
        in_specs=[
            pl.BlockSpec((rows, depth), lambda i: (0, 0)),
            pl.BlockSpec((depth, tile), lambda i: (0, first + i)),
        ],
        out_specs=[
            pl.BlockSpec((rows // 2, tile), lambda i: (0, i)),
            pl.BlockSpec((rows // 2, tile), lambda i: (0, i)),
        ],
        out_shape=[
            jax.ShapeDtypeStruct((rows // 2, columns), bf16),
            jax.ShapeDtypeStruct((rows // 2, columns), bf16),
        ],
        compiler_params=pltpu.CompilerParams(vmem_limit_bytes=large_vmem),
        cost_estimate=pl.CostEstimate(
            flops=2 * rows * depth * columns, bytes_accessed=2 * depth * columns, transcendentals=0
        ),
        name="out_proj",
    )(values, w_out)


def gated_kernel(layout, start, tile, first, last, width, *refs):
    pieces = 1 + max(p for p, _ in layout)
    refs = list(refs)
    order_ref = refs.pop(0)
    x_refs = [refs.pop(0) for _ in range(pieces)]
    gain_ref, gate_ref, up_ref = refs.pop(0), refs.pop(0), refs.pop(0)
    if not first:
        acc_in, square_in = refs.pop(0), refs.pop(0)
    if last:
        out_ref, scaled_ref, ordered = refs
    else:
        acc_ref, square_ref, scaled_ref = refs
    block, lanes = 16, 128
    columns = x_refs[0].shape[1]
    hidden = gate_ref.shape[1]

    squares = None if first else square_in[...]
    for k in range(0, columns, tile):
        wide = jnp.concatenate(
            [x_refs[p][at : at + block, k : k + tile] for p, at in layout], axis=0
        ).astype(f32)
        for j in range(0, tile, lanes):
            part = wide[:, j : j + lanes]
            squares = part * part if squares is None else squares + part * part
        gain = gain_ref[:, start + k : start + k + tile].astype(f32)
        scaled_ref[:, k : k + tile] = (wide * gain).astype(bf16)

    def product(w_ref):
        return jnp.dot(
            scaled_ref[...], w_ref[start : start + columns, :], preferred_element_type=f32
        )

    if not last:
        acc_ref[:, :hidden] = product(gate_ref)
        acc_ref[:, hidden:] = product(up_ref)
        square_ref[...] = squares
        return
    scale = lax.rsqrt(jnp.sum(squares, axis=-1, keepdims=True) * (1.0 / width) + 1e-06)
    gate = (product(gate_ref) + acc_in[:, :hidden]) * scale
    up = (product(up_ref) + acc_in[:, hidden:]) * scale
    active = gate / (1.0 + jnp.exp(-gate)) * up
    for p in range(tp_size):
        at = pl.multiple_of(order_ref[p] * 8, 8)
        for m in range(2):
            begin = p * block + m * 8
            ordered[m, pl.ds(at, 8), :] = active[begin : begin + 8]
    out_ref[...] = ordered[...].astype(bf16)


def gated(order, pieces, layout, gain, gate, up, start, tile, carried, width):
    first = carried is None
    last = not first
    columns = pieces[0].shape[1]
    hidden = gate.shape[1]
    rows = sum(p.shape[0] for p in pieces)
    args = [order] + list(pieces) + [gain, gate, up]
    acc_shape, square_shape = (rows, 2 * hidden), (rows, 128)
    if not first:
        args += list(carried)
    vmem = pl.BlockSpec(memory_space=pltpu.VMEM)
    in_specs = [pl.BlockSpec(memory_space=pltpu.SMEM)] + [vmem] * (len(args) - 1)
    scratch = [pltpu.VMEM((rows, columns), bf16)]
    if last:
        out_dims = (2, rows // 2, hidden)
        out_specs = vmem
        out_shape = jax.ShapeDtypeStruct(out_dims, bf16)
        scratch += [pltpu.VMEM(out_dims, f32)]
    else:
        out_specs = [vmem, vmem]
        out_shape = [jax.ShapeDtypeStruct(acc_shape, f32), jax.ShapeDtypeStruct(square_shape, f32)]
    return pl.pallas_call(
        functools.partial(gated_kernel, layout, start, tile, first, last, width),
        in_specs=in_specs,
        out_specs=out_specs,
        scratch_shapes=scratch,
        out_shape=out_shape,
        compiler_params=pltpu.CompilerParams(vmem_limit_bytes=vmem_limit),
        cost_estimate=pl.CostEstimate(
            flops=4 * rows * columns * hidden,
            bytes_accessed=4 * columns * hidden,
            transcendentals=0,
        ),
        name="gated_pair",
    )(*args)


def shards(
    residual,
    queries,
    latent_cache,
    new_latent,
    lengths,
    positions,
    latent_value_weight,
    w_out,
    norm_gain,
    gate_weight,
    up_weight,
):
    latent = latent_value_weight.shape[1]
    micro, own_rows, width = residual.shape
    block = micro * own_rows
    heads = queries.shape[2]
    me = lax.axis_index("tp")
    my_x, my_z, my_c = me // 4, (me // 2) % 2, me % 2
    order = jnp.stack(
        [
            ((my_x + px) % 4) * 4 + (my_z ^ pz) * 2 + (my_c ^ pc)
            for pc in range(core_size)
            for pz in range(z_size)
            for px in range(x_size)
        ]
    ).astype(jnp.int32)
    tables = rotary_tables(positions.reshape(-1), queries.shape[3] - latent)
    attended = attention(
        queries.reshape((block,) + queries.shape[2:]),
        jnp.swapaxes(latent_cache, 2, 3).reshape(block, latent_cache.shape[3], -1),
        new_latent.reshape(block, -1),
        lengths,
        tables,
        latent,
    )
    arrived = lax.all_to_all(
        attended.reshape(tp_size, heads // tp_size, block, latent),
        "tp",
        split_axis=0,
        concat_axis=0,
        tiled=True,
    )
    cut = 4096
    tile = 1024
    send_b, keep_b, values = value_and_out(
        order, arrived, latent_value_weight, w_out, cut, width - cut, tile
    )
    send_a, keep_a = out_only(values, w_out, block, 0, cut, tile)
    flat_residual = residual.reshape(block, width).astype(f32)

    def add(*parts):
        total = parts[0].astype(f32)
        for part in parts[1:]:
            total = total + part.astype(f32)
        return total

    def x_sum(value, rows):
        right = send(value[rows : 2 * rows], dx=1)
        left = send(value[3 * rows :], dx=3)
        across = send(value[2 * rows : 3 * rows], dx=2)
        return value[:rows], right, left, across

    def x_gather(value):
        return [value, send(value, dx=3), send(value, dx=2), send(value, dx=1)]

    pair_b = add(keep_b, send(send_b, dc=1)).astype(bf16)
    pair_a = add(keep_a, send(send_a, dc=1)).astype(bf16)
    line_b = add(pair_b[: 4 * block], send(pair_b[4 * block :], dz=1)).astype(bf16)
    line_a = add(*x_sum(pair_a, 2 * block))
    line_a = jnp.concatenate(
        [line_a[:block] + flat_residual[:, :cut], line_a[block:]], axis=0
    ).astype(bf16)
    other_a = send(line_a, dz=1)
    both_a = jnp.concatenate(
        [add(line_a[:block], other_a[block:]), add(line_a[block:], other_a[:block])], axis=0
    ).astype(bf16)
    after_a = both_a[:block]
    after_b = add(flat_residual[:, cut:], *x_sum(line_b, block)).astype(bf16)

    near_b = jnp.concatenate(x_gather(after_b), axis=0)
    pieces_a = x_gather(both_a)
    far_b = send(near_b, dz=1)
    pieces_a = pieces_a + [send(g, dc=1) for g in pieces_a]
    near_core_b = send(near_b, dc=1)

    canonical = [
        (pc, pz, px) for pc in range(core_size) for pz in range(z_size) for px in range(x_size)
    ]
    layout_a = [(pc * 4 + px, pz * block) for pc, pz, px in canonical]
    layout_b = [(pc * 2 + pz, px * block) for pc, pz, px in canonical]
    gain_row = norm_gain.reshape(1, width)
    k_tile = 512
    carried = gated(
        order, pieces_a, layout_a, gain_row, gate_weight, up_weight, 0, k_tile, None, width
    )
    pieces_b = [near_b, far_b, near_core_b, send(far_b, dc=1)]
    activation = gated(
        order, pieces_b, layout_b, gain_row, gate_weight, up_weight, cut, k_tile, carried, width
    )
    after_attention = jnp.concatenate([after_a, after_b], axis=1).reshape(residual.shape)
    return (after_attention, activation)


def solution(mesh):
    return jax.shard_map(
        shards,
        mesh=mesh,
        in_specs=(
            P(None, ("dp", "tp"), None),
            P(None, ("dp", "tp"), None, None),
            P(None, ("dp", "tp"), None, None),
            P(None, ("dp", "tp"), None),
            P(None, ("dp", "tp")),
            P(None, ("dp", "tp")),
            P("tp", None, None),
            P("tp", None),
            P(),
            P(None, "tp"),
            P(None, "tp"),
        ),
        out_specs=(P(None, ("dp", "tp"), None), P(None, "dp", "tp")),
        check_vma=False,
    )
```

```python
import functools

import jax
import jax.numpy as jnp
import numpy as np
from jax import lax
from jax.experimental import pallas as pl
from jax.experimental.pallas import tpu as pltpu
from jax.sharding import PartitionSpec as P

score_scale = 192.0 ** (-0.5)
neg_large = -1e30
f32 = jnp.float32
bf16 = jnp.bfloat16
vmem_limit = 20 * 1024 * 1024
large_vmem = 56 * 1024 * 1024
x_size, z_size, core_size = 4, 2, 2
tp_size = x_size * z_size * core_size


flips = {"p": (1, 0, 0), "q": (3, 0, 0), "z": (0, 1, 0), "c": (0, 0, 1)}


def send(value, *dims):
    pairs = []
    for i in range(tp_size):
        x, z, c = i // 4, (i // 2) % 2, i % 2
        for dim in dims:
            fx, fz, fc = flips[dim]
            x, z, c = x ^ fx, z ^ fz, c ^ fc
        pairs.append((i, x * 4 + z * 2 + c))
    return lax.ppermute(value, "tp", pairs)


def rotary_tables(positions, rope):
    half = rope // 2
    exponent = jnp.arange(half, dtype=f32) * (2.0 / rope)
    angles = positions.astype(f32)[..., None] * (10000.0 ** (-exponent))
    cosine, sine = jnp.cos(angles), jnp.sin(angles)
    return jnp.concatenate([cosine, cosine, -sine, sine], axis=-1)


def attention_kernel(
    group, span, latent, len_ref, q_hbm, c_hbm, n_ref, t_ref, out_ref, q_ref, c_ref, held, q_sem, c_sem
):
    count, heads, width = q_ref.shape
    rope = width - latent
    half = rope // 2
    per = len_ref.shape[1]

    copies = []
    for i in range(count // span):
        at = pl.ds(i * span, span)
        copies.append(
            (
                pltpu.make_async_copy(q_hbm.at[at], q_ref.at[at], q_sem.at[i]),
                pltpu.make_async_copy(c_hbm.at[at], c_ref.at[at], c_sem.at[i]),
            )
        )
    for pair in copies:
        for copy in pair:
            copy.start()

    def turn(values, cosine, sine):
        swapped = jnp.concatenate([values[:, half:], values[:, :half]], axis=-1)
        return (values * cosine + swapped * sine).astype(bf16)

    for begin in range(0, count, group):
        scored = []
        for r in range(begin, begin + group):
            if r % span == 0:
                for copy in copies[r // span]:
                    copy.wait()
            table = t_ref[r : r + 1, :]
            cosine, sine = table[:, :rope], table[:, rope:]
            q_lat = q_ref[r, :, :latent]
            q_rope = turn(q_ref[r, :, latent:].astype(f32), cosine, sine)
            n_lat = n_ref[r : r + 1, :latent].astype(f32)
            n_rope = turn(n_ref[r : r + 1, latent:].astype(f32), cosine, sine).astype(f32)
            scores = jnp.dot(q_lat, c_ref[r, :latent, :], preferred_element_type=f32)
            scores += jnp.dot(q_rope, c_ref[r, latent:, :], preferred_element_type=f32)
            own = jnp.sum(q_lat.astype(f32) * n_lat, axis=-1, keepdims=True)
            own += jnp.sum(q_rope.astype(f32) * n_rope, axis=-1, keepdims=True)
            scored.append((scores, own * score_scale, n_lat))
        weighted = []
        for r in range(begin, begin + group):
            scores, own, n_lat = scored[r - begin]
            visible = lax.broadcasted_iota(jnp.int32, scores.shape, 1) < len_ref[r // per, r % per]
            scores = jnp.where(visible, scores * score_scale, neg_large)
            top = jnp.maximum(jnp.max(scores, axis=-1, keepdims=True), own)
            weights = jnp.where(visible, jnp.exp(scores - top), 0.0)
            own_weight = jnp.exp(own - top)
            total = jnp.sum(weights, axis=-1, keepdims=True) + own_weight
            weighted.append((weights.astype(bf16), own_weight, total, n_lat))
        for r in range(begin, begin + group):
            weights, own_weight, total, n_lat = weighted[r - begin]
            context = lax.dot_general(
                weights, c_ref[r, :latent, :], (((1,), (1,)), ((), ())), preferred_element_type=f32
            )
            context += own_weight.astype(bf16).astype(f32) * n_lat
            held[:, r, :] = context * (1.0 / total)
    out_ref[...] = held[...].astype(bf16)


def attention(queries, cache, new_latent, lengths, tables, latent, group=8, span=4):
    count, heads, width = queries.shape
    slots = cache.shape[2]
    vmem = pl.BlockSpec(memory_space=pltpu.VMEM)
    return pl.pallas_call(
        functools.partial(attention_kernel, group, span, latent),
        in_specs=[
            pl.BlockSpec(memory_space=pltpu.SMEM),
            pl.BlockSpec(memory_space=pltpu.HBM),
            pl.BlockSpec(memory_space=pltpu.HBM),
            vmem,
            vmem,
        ],
        out_specs=vmem,
        scratch_shapes=[
            pltpu.VMEM(queries.shape, bf16),
            pltpu.VMEM(cache.shape, bf16),
            pltpu.VMEM((heads, count, latent), f32),
            pltpu.SemaphoreType.DMA((count // span,)),
            pltpu.SemaphoreType.DMA((count // span,)),
        ],
        out_shape=jax.ShapeDtypeStruct((heads, count, latent), bf16),
        compiler_params=pltpu.CompilerParams(vmem_limit_bytes=large_vmem),
        cost_estimate=pl.CostEstimate(
            flops=4 * count * heads * width * slots,
            bytes_accessed=2 * count * width * (heads + slots),
            transcendentals=count * heads * slots,
        ),
        name="attention",
    )(lengths, queries, cache, new_latent, tables)


def out_kernel(block, spans, orders, with_values, *refs):
    refs = list(refs)
    if with_values:
        order_ref, a_ref, v_ref = refs.pop(0), refs.pop(0), refs.pop(0)
    else:
        value_ref = refs.pop(0)
    w_hbm = refs.pop(0)
    outs = [(refs.pop(0), refs.pop(0)) for _ in spans]
    if with_values:
        value_ref = refs.pop(0)
    w_refs = [refs.pop(0) for _ in spans]
    if with_values:
        gathered = refs.pop(0)
    sem = refs.pop(0)
    copies = []
    for i, (begin, columns) in enumerate(spans):
        copies.append(
            pltpu.make_async_copy(w_hbm.at[:, begin : begin + columns], w_refs[i], sem.at[i])
        )
        copies[i].start()
    if with_values:
        for p in range(tp_size):
            gathered[:, p * block : (p + 1) * block, :] = a_ref[order_ref[p]]
        heads, width = v_ref.shape[0], v_ref.shape[2]
        for h in range(heads):
            value_ref[:, h * width : (h + 1) * width] = jnp.dot(
                gathered[h], v_ref[h], preferred_element_type=f32
            ).astype(bf16)
    values = value_ref[...]
    half = values.shape[0] // 2
    for i in range(len(spans)):
        rows = jnp.concatenate([values[p * block : (p + 1) * block] for p in orders[i]], axis=0)
        copies[i].wait()
        result = jnp.dot(rows, w_refs[i][...], preferred_element_type=f32).astype(bf16)
        outs[i][0][...] = result[:half]
        outs[i][1][...] = result[half:]


def project(order, source, value_weight, w_out, block, spans, orders):
    with_values = value_weight is not None
    depth = w_out.shape[0]
    rows = tp_size * block
    vmem = pl.BlockSpec(memory_space=pltpu.VMEM)
    args, in_specs = [source], [vmem]
    if with_values:
        args, in_specs = [order, source, value_weight], [
            pl.BlockSpec(memory_space=pltpu.SMEM),
            vmem,
            vmem,
        ]
    out_shape = []
    for _, columns in spans:
        out_shape += [jax.ShapeDtypeStruct((rows // 2, columns), bf16)] * 2
    scratch = [pltpu.VMEM((depth, columns), bf16) for _, columns in spans]
    if with_values:
        out_shape.append(jax.ShapeDtypeStruct((rows, depth), bf16))
        scratch.append(pltpu.VMEM((source.shape[1], rows, source.shape[3]), bf16))
    total = sum(columns for _, columns in spans)
    return pl.pallas_call(
        functools.partial(out_kernel, block, spans, orders, with_values),
        in_specs=in_specs + [pl.BlockSpec(memory_space=pltpu.HBM)],
        out_specs=[vmem] * len(out_shape),
        out_shape=out_shape,
        scratch_shapes=scratch + [pltpu.SemaphoreType.DMA((len(spans),))],
        compiler_params=pltpu.CompilerParams(vmem_limit_bytes=vmem_limit),
        cost_estimate=pl.CostEstimate(
            flops=2 * rows * depth * total, bytes_accessed=2 * depth * total, transcendentals=0
        ),
        name="out_proj",
    )(*args, w_out)


def gated_kernel(spans, layouts, block, *refs):
    refs = list(refs)
    order_ref = refs.pop(0)
    x_refs = [[refs.pop(0) for _ in range(4)] for _ in spans]
    gain_ref, gate_ref, up_ref, out_ref, ordered = refs
    lanes = 128
    squares = gate = up = None
    for (begin, columns), pieces, layout in zip(spans, x_refs, layouts):
        wide = jnp.concatenate(
            [pieces[p][at : at + block, :] for p, at in layout], axis=0
        ).astype(f32)
        for j in range(0, columns, lanes):
            part = wide[:, j : j + lanes]
            squares = part * part if squares is None else squares + part * part
        gain = gain_ref[:, begin : begin + columns].astype(f32)
        scaled = (wide * gain).astype(bf16)

        def product(w_ref):
            return jnp.dot(scaled, w_ref[begin : begin + columns, :], preferred_element_type=f32)

        gate = product(gate_ref) if gate is None else gate + product(gate_ref)
        up = product(up_ref) if up is None else up + product(up_ref)
    width = gate_ref.shape[0]
    scale = lax.rsqrt(jnp.sum(squares, axis=-1, keepdims=True) * (1.0 / width) + 1e-06)
    gate, up = gate * scale, up * scale
    active = gate / (1.0 + jnp.exp(-gate)) * up
    own = out_ref.shape[1] // tp_size
    for p in range(tp_size):
        at = pl.multiple_of(order_ref[p] * own, own)
        for m in range(out_ref.shape[0]):
            start = p * block + m * own
            ordered[m, pl.ds(at, own), :] = active[start : start + own]
    out_ref[...] = ordered[...].astype(bf16)


def gated(order, pieces, spans, layouts, block, gain, gate, up, micro):
    columns, hidden = gate.shape
    rows = tp_size * block
    out_dims = (micro, rows // micro, hidden)
    vmem = pl.BlockSpec(memory_space=pltpu.VMEM)
    args = [piece for stream in pieces for piece in stream] + [gain, gate, up]
    return pl.pallas_call(
        functools.partial(gated_kernel, spans, layouts, block),
        in_specs=[pl.BlockSpec(memory_space=pltpu.SMEM)] + [vmem] * len(args),
        out_specs=vmem,
        out_shape=jax.ShapeDtypeStruct(out_dims, bf16),
        scratch_shapes=[pltpu.VMEM(out_dims, f32)],
        compiler_params=pltpu.CompilerParams(vmem_limit_bytes=vmem_limit),
        cost_estimate=pl.CostEstimate(
            flops=4 * rows * columns * hidden,
            bytes_accessed=4 * columns * hidden,
            transcendentals=0,
        ),
        name="gated_pair",
    )(order, *args)


def add(*parts):
    total = parts[0].astype(f32)
    for part in parts[1:]:
        total = total + part.astype(f32)
    return total


def shards(
    residual,
    queries,
    latent_cache,
    new_latent,
    lengths,
    positions,
    latent_value_weight,
    w_out,
    norm_gain,
    gate_weight,
    up_weight,
):
    latent = latent_value_weight.shape[1]
    micro, own_rows, width = residual.shape
    block = micro * own_rows
    heads = queries.shape[2]
    me = lax.axis_index("tp")
    places = [(c, p, q, z) for c in range(2) for p in range(2) for q in range(2) for z in range(2)]
    order = jnp.stack(
        [((me // 4) ^ p ^ (3 * q)) * 4 + (((me // 2) % 2) ^ z) * 2 + ((me % 2) ^ c) for c, p, q, z in places]
    ).astype(jnp.int32)
    tables = rotary_tables(positions.reshape(-1), queries.shape[3] - latent)
    attended = attention(
        queries.reshape((block,) + queries.shape[2:]),
        jnp.swapaxes(latent_cache, 2, 3).reshape(block, latent_cache.shape[3], -1),
        new_latent.reshape(block, -1),
        lengths,
        tables,
        latent,
    )
    arrived = lax.all_to_all(
        attended.reshape(tp_size, heads // tp_size, block, latent),
        "tp",
        split_axis=0,
        concat_axis=0,
        tiled=True,
    )

    streams = ("pqz", "qzp", "zpq")
    third = -(-width // (3 * 128)) * 128
    spans = [(i * third, min(third, width - i * third)) for i in range(3)]
    names = "cpqz"
    orders, layouts = [], []
    for dims in streams:
        rank = [names.index(d) for d in "c" + dims]
        orders.append(sorted(range(tp_size), key=lambda i: [places[i][k] for k in rank]))
        layouts.append(
            [
                (at[rank[0]] * 2 + at[rank[1]], (at[rank[2]] * 2 + at[rank[3]]) * block)
                for at in places
            ]
        )
    keep_0, send_0, values = project(
        order, arrived, latent_value_weight, w_out, block, spans[:1], orders[:1]
    )
    keep_1, send_1, keep_2, send_2 = project(
        order, values, None, w_out, block, spans[1:], orders[1:]
    )
    kept, sent = [keep_0, keep_1, keep_2], [send_0, send_1, send_2]
    flat_residual = residual.reshape(block, width)

    each = range(3)
    pair = [add(kept[i], send(sent[i], "c")).astype(bf16) for i in each]
    four = [
        add(pair[i][: 4 * block], send(pair[i][4 * block :], streams[i][0])).astype(bf16)
        for i in each
    ]
    two = []
    for i in each:
        total = add(four[i][: 2 * block], send(four[i][2 * block :], streams[i][1]))
        begin, columns = spans[i]
        own = total[:block] + flat_residual[:, begin : begin + columns].astype(f32)
        two.append(jnp.concatenate([own, total[block:]], axis=0).astype(bf16))
    other = [send(two[i], streams[i][2]) for i in each]
    both = [
        jnp.concatenate(
            [add(two[i][:block], other[i][block:]), add(two[i][block:], other[i][:block])], axis=0
        ).astype(bf16)
        for i in each
    ]
    near = [jnp.concatenate([both[i], send(both[i], streams[i][1])], axis=0) for i in each]
    far = [send(near[i], streams[i][0]) for i in each]
    pieces = [[near[i], far[i], send(near[i], "c"), send(far[i], "c")] for i in each]
    activation = gated(
        order,
        pieces,
        spans,
        layouts,
        block,
        norm_gain.reshape(1, width),
        gate_weight,
        up_weight,
        micro,
    )
    after_attention = jnp.concatenate([both[i][:block] for i in each], axis=1)
    return (after_attention.reshape(residual.shape), activation)


def solution(mesh):
    return jax.shard_map(
        shards,
        mesh=mesh,
        in_specs=(
            P(None, ("dp", "tp"), None),
            P(None, ("dp", "tp"), None, None),
            P(None, ("dp", "tp"), None, None),
            P(None, ("dp", "tp"), None),
            P(None, ("dp", "tp")),
            P(None, ("dp", "tp")),
            P("tp", None, None),
            P("tp", None),
            P(),
            P(None, "tp"),
            P(None, "tp"),
        ),
        out_specs=(P(None, ("dp", "tp"), None), P(None, "dp", "tp")),
        check_vma=False,
    )
```

```python
import functools

import jax
import jax.numpy as jnp
import numpy as np
from jax import lax
from jax.experimental import pallas as pl
from jax.experimental.pallas import tpu as pltpu
from jax.sharding import PartitionSpec as P

score_scale = 192.0 ** (-0.5)
neg_large = -1e30
f32 = jnp.float32
bf16 = jnp.bfloat16
vmem_limit = 20 * 1024 * 1024
large_vmem = 56 * 1024 * 1024
x_size, z_size, core_size = 4, 2, 2
tp_size = x_size * z_size * core_size
stream_sets = 1


flips = {"p": (1, 0, 0), "q": (3, 0, 0), "z": (0, 1, 0), "c": (0, 0, 1)}


def send(value, *dims):
    pairs = []
    for i in range(tp_size):
        x, z, c = i // 4, (i // 2) % 2, i % 2
        for dim in dims:
            fx, fz, fc = flips[dim]
            x, z, c = x ^ fx, z ^ fz, c ^ fc
        pairs.append((i, x * 4 + z * 2 + c))
    return lax.ppermute(value, "tp", pairs)


def rotary_frequencies(rope):
    exponent = np.arange(rope // 2) * (2.0 / rope)
    return jnp.asarray(np.tile(10000.0**-exponent, 2)[None, :], f32)


def attention_kernel(
    group, span, latent, len_ref, pos_ref, q_hbm, c_hbm, n_ref, f_ref, out_ref, q_ref, c_ref, held, q_sem, c_sem
):
    count, heads, width = q_ref.shape
    rope = width - latent
    half = rope // 2
    per = len_ref.shape[1]

    copies = []
    for i in range(count // span):
        at = pl.ds(i * span, span)
        copies.append(
            (
                pltpu.make_async_copy(q_hbm.at[at], q_ref.at[at], q_sem.at[i]),
                pltpu.make_async_copy(c_hbm.at[at], c_ref.at[at], c_sem.at[i]),
            )
        )
    for pair in copies:
        for copy in pair:
            copy.start()

    row_ids = lax.broadcasted_iota(jnp.int32, (count, rope), 0)
    positions = jnp.zeros((count, rope), f32)
    for r in range(count):
        positions = jnp.where(row_ids == r, pos_ref[r // per, r % per].astype(f32), positions)
    angles = positions * f_ref[...]
    cosines, sines = jnp.cos(angles), jnp.sin(angles)
    leading = lax.broadcasted_iota(jnp.int32, (count, rope), 1) < half
    sines = jnp.where(leading, -sines, sines)

    def turn(values, cosine, sine):
        swapped = jnp.concatenate([values[:, half:], values[:, :half]], axis=-1)
        return (values * cosine + swapped * sine).astype(bf16)

    for begin in range(0, count, group):
        scored = []
        for r in range(begin, begin + group):
            if r % span == 0:
                for copy in copies[r // span]:
                    copy.wait()
            cosine, sine = cosines[r : r + 1], sines[r : r + 1]
            q_lat = q_ref[r, :, :latent]
            q_rope = turn(q_ref[r, :, latent:].astype(f32), cosine, sine)
            n_lat = n_ref[r : r + 1, :latent].astype(f32)
            n_rope = turn(n_ref[r : r + 1, latent:].astype(f32), cosine, sine).astype(f32)
            scores = jnp.dot(q_lat, c_ref[r, :latent, :], preferred_element_type=f32)
            scores += jnp.dot(q_rope, c_ref[r, latent:, :], preferred_element_type=f32)
            own = jnp.sum(q_lat.astype(f32) * n_lat, axis=-1, keepdims=True)
            own += jnp.sum(q_rope.astype(f32) * n_rope, axis=-1, keepdims=True)
            scored.append((scores, own * score_scale, n_lat))
        weighted = []
        for r in range(begin, begin + group):
            scores, own, n_lat = scored[r - begin]
            visible = lax.broadcasted_iota(jnp.int32, scores.shape, 1) < len_ref[r // per, r % per]
            scores = jnp.where(visible, scores * score_scale, neg_large)
            top = jnp.maximum(jnp.max(scores, axis=-1, keepdims=True), own)
            weights = jnp.where(visible, jnp.exp(scores - top), 0.0)
            own_weight = jnp.exp(own - top)
            total = jnp.sum(weights, axis=-1, keepdims=True) + own_weight
            weighted.append((weights.astype(bf16), own_weight, total, n_lat))
        for r in range(begin, begin + group):
            weights, own_weight, total, n_lat = weighted[r - begin]
            context = lax.dot_general(
                weights, c_ref[r, :latent, :], (((1,), (1,)), ((), ())), preferred_element_type=f32
            )
            context += own_weight.astype(bf16).astype(f32) * n_lat
            held[:, r, :] = context * (1.0 / total)
    out_ref[...] = held[...].astype(bf16)


def attention(queries, cache, new_latent, lengths, positions, latent, group=8, span=4):
    count, heads, width = queries.shape
    slots = cache.shape[2]
    vmem = pl.BlockSpec(memory_space=pltpu.VMEM)
    return pl.pallas_call(
        functools.partial(attention_kernel, group, span, latent),
        in_specs=[
            pl.BlockSpec(memory_space=pltpu.SMEM),
            pl.BlockSpec(memory_space=pltpu.SMEM),
            pl.BlockSpec(memory_space=pltpu.HBM),
            pl.BlockSpec(memory_space=pltpu.HBM),
            vmem,
            vmem,
        ],
        out_specs=vmem,
        scratch_shapes=[
            pltpu.VMEM(queries.shape, bf16),
            pltpu.VMEM(cache.shape, bf16),
            pltpu.VMEM((heads, count, latent), f32),
            pltpu.SemaphoreType.DMA((count // span,)),
            pltpu.SemaphoreType.DMA((count // span,)),
        ],
        out_shape=jax.ShapeDtypeStruct((heads, count, latent), bf16),
        compiler_params=pltpu.CompilerParams(vmem_limit_bytes=large_vmem),
        cost_estimate=pl.CostEstimate(
            flops=4 * count * heads * width * slots,
            bytes_accessed=2 * count * width * (heads + slots),
            transcendentals=count * heads * slots,
        ),
        name="attention",
    )(lengths, positions, queries, cache, new_latent, rotary_frequencies(width - latent))


def value_kernel(block, order_ref, a_ref, v_ref, value_ref, gathered):
    for p in range(tp_size):
        gathered[:, p * block : (p + 1) * block, :] = a_ref[order_ref[p]]
    heads, width = v_ref.shape[0], v_ref.shape[2]
    for h in range(heads):
        value_ref[:, h * width : (h + 1) * width] = jnp.dot(
            gathered[h], v_ref[h], preferred_element_type=f32
        ).astype(bf16)


def value_rows(order, arrived, value_weight):
    sources, heads, block, latent = arrived.shape
    rows, depth = sources * block, heads * value_weight.shape[2]
    vmem = pl.BlockSpec(memory_space=pltpu.VMEM)
    return pl.pallas_call(
        functools.partial(value_kernel, block),
        in_specs=[pl.BlockSpec(memory_space=pltpu.SMEM), vmem, vmem],
        out_specs=vmem,
        out_shape=jax.ShapeDtypeStruct((rows, depth), bf16),
        scratch_shapes=[pltpu.VMEM((heads, rows, latent), bf16)],
        compiler_params=pltpu.CompilerParams(vmem_limit_bytes=vmem_limit),
        cost_estimate=pl.CostEstimate(
            flops=2 * rows * depth * latent, bytes_accessed=4 * rows * depth, transcendentals=0
        ),
        name="value_rows",
    )(order, arrived, value_weight)


def out_kernel(block, spans, orders, value_ref, w_ref, *out_refs):
    values = value_ref[...]
    half = values.shape[0] // 2
    for i, (begin, columns) in enumerate(spans):
        rows = jnp.concatenate([values[p * block : (p + 1) * block] for p in orders[i]], axis=0)
        result = jnp.dot(
            rows, w_ref[:, begin : begin + columns], preferred_element_type=f32
        ).astype(bf16)
        out_refs[2 * i][...] = result[:half]
        out_refs[2 * i + 1][...] = result[half:]


def project(values, w_out, block, spans, orders):
    rows, depth = values.shape
    width = w_out.shape[1]
    vmem = pl.BlockSpec(memory_space=pltpu.VMEM)
    out_shape = []
    for _, columns in spans:
        out_shape += [jax.ShapeDtypeStruct((rows // 2, columns), bf16)] * 2
    return pl.pallas_call(
        functools.partial(out_kernel, block, spans, orders),
        in_specs=[vmem, vmem],
        out_specs=[vmem] * len(out_shape),
        out_shape=out_shape,
        compiler_params=pltpu.CompilerParams(vmem_limit_bytes=vmem_limit),
        cost_estimate=pl.CostEstimate(
            flops=2 * rows * depth * width, bytes_accessed=2 * depth * width, transcendentals=0
        ),
        name="out_proj",
    )(values, w_out)


def gated_kernel(spans, layouts, block, last, *refs):
    refs = list(refs)
    if last:
        order_ref = refs.pop(0)
    x_refs = [[refs.pop(0) for _ in range(2)] for _ in spans]
    gain_ref, gate_ref, up_ref = refs.pop(0), refs.pop(0), refs.pop(0)
    if last:
        acc_in, square_in, out_ref, ordered = refs
    else:
        acc_ref, square_ref = refs
    lanes = 128
    hidden = gate_ref.shape[1]
    squares, gates, ups = ([[] for _ in range(tp_size)] for _ in range(3))
    for (begin, columns), pieces, layout in zip(spans, x_refs, layouts):
        wide = jnp.concatenate(
            [pieces[p][at : at + block, :] for _, p, at in layout], axis=0
        ).astype(f32)
        square = None
        for j in range(0, columns, lanes):
            part = wide[:, j : j + lanes]
            square = part * part if square is None else square + part * part
        gain = gain_ref[:, begin : begin + columns].astype(f32)
        scaled = (wide * gain).astype(bf16)
        gate = jnp.dot(scaled, gate_ref[begin : begin + columns, :], preferred_element_type=f32)
        up = jnp.dot(scaled, up_ref[begin : begin + columns, :], preferred_element_type=f32)
        for i, (place, _, _) in enumerate(layout):
            rows = slice(i * block, (i + 1) * block)
            squares[place].append(square[rows])
            gates[place].append(gate[rows])
            ups[place].append(up[rows])

    for place in range(tp_size):
        rows = slice(place * block, (place + 1) * block)
        if last:
            squares[place].append(square_in[rows, :])
            gates[place].append(acc_in[rows, :hidden])
            ups[place].append(acc_in[rows, hidden:])
        elif not gates[place]:
            squares[place].append(jnp.zeros((block, lanes), f32))
            gates[place].append(jnp.zeros((block, hidden), f32))
            ups[place].append(jnp.zeros((block, hidden), f32))
        square, gate, up = (add(*found[place]) for found in (squares, gates, ups))
        if not last:
            square_ref[rows, :] = square
            acc_ref[rows, :hidden] = gate
            acc_ref[rows, hidden:] = up
            continue
        mean = jnp.sum(square, axis=-1, keepdims=True) * (1.0 / gate_ref.shape[0])
        scale = lax.rsqrt(mean + 1e-06)
        gate, up = gate * scale, up * scale
        active = gate / (1.0 + jnp.exp(-gate)) * up
        own = out_ref.shape[1] // tp_size
        at = pl.multiple_of(order_ref[place] * own, own)
        for m in range(out_ref.shape[0]):
            ordered[m, pl.ds(at, own), :] = active[m * own : (m + 1) * own]
    if last:
        out_ref[...] = ordered[...].astype(bf16)


def gated(order, pieces, spans, layouts, block, gain, gate, up, micro, carried):
    columns, hidden = gate.shape
    rows = tp_size * block
    last = carried is not None
    vmem = pl.BlockSpec(memory_space=pltpu.VMEM)
    args = [piece for stream in pieces for piece in stream] + [gain, gate, up]
    in_specs = [vmem] * len(args)
    if last:
        args = [order] + args + list(carried)
        in_specs = [pl.BlockSpec(memory_space=pltpu.SMEM)] + in_specs + [vmem] * 2
        out_dims = (micro, rows // micro, hidden)
        out_shape = jax.ShapeDtypeStruct(out_dims, bf16)
        out_specs, scratch = vmem, [pltpu.VMEM(out_dims, f32)]
    else:
        out_shape = [
            jax.ShapeDtypeStruct((rows, 2 * hidden), f32),
            jax.ShapeDtypeStruct((rows, 128), f32),
        ]
        out_specs, scratch = [vmem, vmem], []
    return pl.pallas_call(
        functools.partial(gated_kernel, spans, layouts, block, last),
        in_specs=in_specs,
        out_specs=out_specs,
        out_shape=out_shape,
        scratch_shapes=scratch,
        compiler_params=pltpu.CompilerParams(vmem_limit_bytes=vmem_limit),
        cost_estimate=pl.CostEstimate(
            flops=2 * rows * columns * hidden,
            bytes_accessed=4 * columns * hidden,
            transcendentals=0,
        ),
        name="gated_far" if last else "gated_near",
    )(*args)


def add(*parts):
    total = parts[0].astype(f32)
    for part in parts[1:]:
        total = total + part.astype(f32)
    return total


def shards(
    residual,
    queries,
    latent_cache,
    new_latent,
    lengths,
    positions,
    latent_value_weight,
    w_out,
    norm_gain,
    gate_weight,
    up_weight,
):
    latent = latent_value_weight.shape[1]
    micro, own_rows, width = residual.shape
    block = micro * own_rows
    heads = queries.shape[2]
    me = lax.axis_index("tp")
    places = [(c, p, q, z) for c in range(2) for p in range(2) for q in range(2) for z in range(2)]
    order = jnp.stack(
        [((me // 4) ^ p ^ (3 * q)) * 4 + (((me // 2) % 2) ^ z) * 2 + ((me % 2) ^ c) for c, p, q, z in places]
    ).astype(jnp.int32)
    attended = attention(
        queries.reshape((block,) + queries.shape[2:]),
        jnp.swapaxes(latent_cache, 2, 3).reshape(block, latent_cache.shape[3], -1),
        new_latent.reshape(block, -1),
        lengths,
        positions,
        latent,
    )
    arrived = lax.all_to_all(
        attended.reshape(tp_size, heads // tp_size, block, latent),
        "tp",
        split_axis=0,
        concat_axis=0,
        tiled=True,
    )

    streams = ("pqz", "qzp", "zpq") * stream_sets
    each = range(len(streams))
    step = -(-width // (len(streams) * 128)) * 128
    spans = [(i * step, min(step, width - i * step)) for i in each]
    names = "cpqz"
    orders, layouts = [], []
    for dims in streams:
        rank = [names.index(d) for d in "c" + dims]
        orders.append(sorted(range(tp_size), key=lambda i: [places[i][k] for k in rank]))
        layouts.append(
            [
                [
                    (i, at[rank[0]], (at[rank[2]] * 2 + at[rank[3]]) * block)
                    for i, at in enumerate(places)
                    if at[rank[1]] == side
                ]
                for side in range(2)
            ]
        )
    values = value_rows(order, arrived, latent_value_weight)
    projected = project(values, w_out, block, spans, orders)
    kept, sent = projected[0::2], projected[1::2]
    flat_residual = residual.reshape(block, width)

    pair = [add(kept[i], send(sent[i], "c")).astype(bf16) for i in each]
    four = [
        add(pair[i][: 4 * block], send(pair[i][4 * block :], streams[i][0])).astype(bf16)
        for i in each
    ]
    two = []
    for i in each:
        total = add(four[i][: 2 * block], send(four[i][2 * block :], streams[i][1]))
        begin, columns = spans[i]
        own = total[:block] + flat_residual[:, begin : begin + columns].astype(f32)
        two.append(jnp.concatenate([own, total[block:]], axis=0).astype(bf16))
    other = [send(two[i], streams[i][2]) for i in each]
    both = [
        jnp.concatenate(
            [add(two[i][:block], other[i][block:]), add(two[i][block:], other[i][:block])], axis=0
        ).astype(bf16)
        for i in each
    ]
    near = [jnp.concatenate([both[i], send(both[i], streams[i][1])], axis=0) for i in each]
    far = [send(near[i], streams[i][0]) for i in each]
    def products(sides, side, carried):
        return gated(
            order,
            [[sides[i], send(sides[i], "c")] for i in each],
            spans,
            [layout[side] for layout in layouts],
            block,
            norm_gain.reshape(1, width),
            gate_weight,
            up_weight,
            micro,
            carried,
        )

    carried = products(near, 0, None)
    far, carried = lax.optimization_barrier((far, carried))
    activation = products(far, 1, carried)
    after_attention = jnp.concatenate([both[i][:block] for i in each], axis=1)
    return (after_attention.reshape(residual.shape), activation)


def solution(mesh):
    return jax.shard_map(
        shards,
        mesh=mesh,
        in_specs=(
            P(None, ("dp", "tp"), None),
            P(None, ("dp", "tp"), None, None),
            P(None, ("dp", "tp"), None, None),
            P(None, ("dp", "tp"), None),
            P(None, ("dp", "tp")),
            P(None, ("dp", "tp")),
            P("tp", None, None),
            P("tp", None),
            P(),
            P(None, "tp"),
            P(None, "tp"),
        ),
        out_specs=(P(None, ("dp", "tp"), None), P(None, "dp", "tp")),
        check_vma=False,
    )
```

```python
import functools

import jax
import jax.numpy as jnp
import numpy as np
from jax import lax
from jax.experimental import pallas as pl
from jax.experimental.pallas import tpu as pltpu
from jax.sharding import PartitionSpec as P

score_scale = 192.0 ** (-0.5)
neg_large = -1e30
f32 = jnp.float32
bf16 = jnp.bfloat16
vmem_limit = 20 * 1024 * 1024
large_vmem = 56 * 1024 * 1024
x_size, z_size, core_size = 4, 2, 2
tp_size = x_size * z_size * core_size


flips = {"p": (1, 0, 0), "q": (3, 0, 0), "z": (0, 1, 0), "c": (0, 0, 1)}


def send(value, *dims):
    pairs = []
    for i in range(tp_size):
        x, z, c = i // 4, (i // 2) % 2, i % 2
        for dim in dims:
            fx, fz, fc = flips[dim]
            x, z, c = x ^ fx, z ^ fz, c ^ fc
        pairs.append((i, x * 4 + z * 2 + c))
    return lax.ppermute(value, "tp", pairs)


def rotary_frequencies(rope):
    exponent = np.arange(rope // 2) * (2.0 / rope)
    return jnp.asarray(np.tile(10000.0**-exponent, 2)[None, :], f32)


def attention_kernel(
    group, span, latent, len_ref, pos_ref, q_hbm, c_hbm, n_ref, f_ref, out_ref, q_ref, c_ref, held, q_sem, c_sem
):
    count, heads, width = q_ref.shape
    rope = width - latent
    half = rope // 2
    per = len_ref.shape[1]

    copies = []
    for i in range(count // span):
        at = pl.ds(i * span, span)
        copies.append(
            (
                pltpu.make_async_copy(q_hbm.at[at], q_ref.at[at], q_sem.at[i]),
                pltpu.make_async_copy(c_hbm.at[at], c_ref.at[at], c_sem.at[i]),
            )
        )
    for pair in copies:
        for copy in pair:
            copy.start()

    row_ids = lax.broadcasted_iota(jnp.int32, (count, rope), 0)
    positions = jnp.zeros((count, rope), f32)
    for r in range(count):
        positions = jnp.where(row_ids == r, pos_ref[r // per, r % per].astype(f32), positions)
    angles = positions * f_ref[...]
    cosines, sines = jnp.cos(angles), jnp.sin(angles)
    leading = lax.broadcasted_iota(jnp.int32, (count, rope), 1) < half
    sines = jnp.where(leading, -sines, sines)

    def turn(values, cosine, sine):
        swapped = jnp.concatenate([values[:, half:], values[:, :half]], axis=-1)
        return (values * cosine + swapped * sine).astype(bf16)

    for begin in range(0, count, group):
        scored = []
        for r in range(begin, begin + group):
            if r % span == 0:
                for copy in copies[r // span]:
                    copy.wait()
            cosine, sine = cosines[r : r + 1], sines[r : r + 1]
            q_lat = q_ref[r, :, :latent]
            q_rope = turn(q_ref[r, :, latent:].astype(f32), cosine, sine)
            n_lat = n_ref[r : r + 1, :latent].astype(f32)
            n_rope = turn(n_ref[r : r + 1, latent:].astype(f32), cosine, sine).astype(f32)
            scores = jnp.dot(q_lat, c_ref[r, :latent, :], preferred_element_type=f32)
            scores += jnp.dot(q_rope, c_ref[r, latent:, :], preferred_element_type=f32)
            own = jnp.sum(q_lat.astype(f32) * n_lat, axis=-1, keepdims=True)
            own += jnp.sum(q_rope.astype(f32) * n_rope, axis=-1, keepdims=True)
            scored.append((scores, own * score_scale, n_lat))
        weighted = []
        for r in range(begin, begin + group):
            scores, own, n_lat = scored[r - begin]
            visible = lax.broadcasted_iota(jnp.int32, scores.shape, 1) < len_ref[r // per, r % per]
            scores = jnp.where(visible, scores * score_scale, neg_large)
            top = jnp.maximum(jnp.max(scores, axis=-1, keepdims=True), own)
            weights = jnp.where(visible, jnp.exp(scores - top), 0.0)
            own_weight = jnp.exp(own - top)
            total = jnp.sum(weights, axis=-1, keepdims=True) + own_weight
            weighted.append((weights.astype(bf16), own_weight, total, n_lat))
        for r in range(begin, begin + group):
            weights, own_weight, total, n_lat = weighted[r - begin]
            context = lax.dot_general(
                weights, c_ref[r, :latent, :], (((1,), (1,)), ((), ())), preferred_element_type=f32
            )
            context += own_weight.astype(bf16).astype(f32) * n_lat
            held[:, r, :] = context * (1.0 / total)
    out_ref[...] = held[...].astype(bf16)


def attention(queries, cache, new_latent, lengths, positions, latent, group=8, span=4):
    count, heads, width = queries.shape
    slots = cache.shape[2]
    vmem = pl.BlockSpec(memory_space=pltpu.VMEM)
    return pl.pallas_call(
        functools.partial(attention_kernel, group, span, latent),
        in_specs=[
            pl.BlockSpec(memory_space=pltpu.SMEM),
            pl.BlockSpec(memory_space=pltpu.SMEM),
            pl.BlockSpec(memory_space=pltpu.HBM),
            pl.BlockSpec(memory_space=pltpu.HBM),
            vmem,
            vmem,
        ],
        out_specs=vmem,
        scratch_shapes=[
            pltpu.VMEM(queries.shape, bf16),
            pltpu.VMEM(cache.shape, bf16),
            pltpu.VMEM((heads, count, latent), f32),
            pltpu.SemaphoreType.DMA((count // span,)),
            pltpu.SemaphoreType.DMA((count // span,)),
        ],
        out_shape=jax.ShapeDtypeStruct((heads, count, latent), bf16),
        compiler_params=pltpu.CompilerParams(vmem_limit_bytes=large_vmem),
        cost_estimate=pl.CostEstimate(
            flops=4 * count * heads * width * slots,
            bytes_accessed=2 * count * width * (heads + slots),
            transcendentals=count * heads * slots,
        ),
        name="attention",
    )(lengths, positions, queries, cache, new_latent, rotary_frequencies(width - latent))


def value_kernel(block, order_ref, a_ref, v_ref, value_ref, gathered):
    for p in range(tp_size):
        gathered[:, p * block : (p + 1) * block, :] = a_ref[order_ref[p]]
    heads, width = v_ref.shape[0], v_ref.shape[2]
    for h in range(heads):
        value_ref[:, h * width : (h + 1) * width] = jnp.dot(
            gathered[h], v_ref[h], preferred_element_type=f32
        ).astype(bf16)


def value_rows(order, arrived, value_weight):
    sources, heads, block, latent = arrived.shape
    rows, depth = sources * block, heads * value_weight.shape[2]
    vmem = pl.BlockSpec(memory_space=pltpu.VMEM)
    return pl.pallas_call(
        functools.partial(value_kernel, block),
        in_specs=[pl.BlockSpec(memory_space=pltpu.SMEM), vmem, vmem],
        out_specs=vmem,
        out_shape=jax.ShapeDtypeStruct((rows, depth), bf16),
        scratch_shapes=[pltpu.VMEM((heads, rows, latent), bf16)],
        compiler_params=pltpu.CompilerParams(vmem_limit_bytes=vmem_limit),
        cost_estimate=pl.CostEstimate(
            flops=32 * rows * depth * latent, bytes_accessed=32 * rows * depth, transcendentals=0
        ),
        name="value_rows",
    )(order, arrived, value_weight)


def out_kernel(block, spans, orders, value_ref, w_ref, *out_refs):
    values = value_ref[...]
    half = values.shape[0] // 2
    for i, (begin, columns) in enumerate(spans):
        rows = jnp.concatenate([values[p * block : (p + 1) * block] for p in orders[i]], axis=0)
        result = jnp.dot(
            rows, w_ref[:, begin : begin + columns], preferred_element_type=f32
        ).astype(bf16)
        out_refs[2 * i][...] = result[:half]
        out_refs[2 * i + 1][...] = result[half:]


def project(values, w_out, block, spans, orders):
    rows, depth = values.shape
    width = w_out.shape[1]
    vmem = pl.BlockSpec(memory_space=pltpu.VMEM)
    out_shape = []
    for _, columns in spans:
        out_shape += [jax.ShapeDtypeStruct((rows // 2, columns), bf16)] * 2
    return pl.pallas_call(
        functools.partial(out_kernel, block, spans, orders),
        in_specs=[vmem, vmem],
        out_specs=[vmem] * len(out_shape),
        out_shape=out_shape,
        compiler_params=pltpu.CompilerParams(vmem_limit_bytes=vmem_limit),
        cost_estimate=pl.CostEstimate(
            flops=2 * rows * depth * width, bytes_accessed=2 * depth * width, transcendentals=0
        ),
        name="out_proj",
    )(values, w_out)


def gated_kernel(spans, layouts, block, last, *refs):
    refs = list(refs)
    if last:
        order_ref = refs.pop(0)
    x_refs = [[refs.pop(0) for _ in range(2)] for _ in spans]
    gain_ref, gate_ref, up_ref = refs.pop(0), refs.pop(0), refs.pop(0)
    if last:
        acc_in, square_in, out_ref, ordered = refs
    else:
        acc_ref, square_ref = refs
    lanes = 128
    hidden = gate_ref.shape[1]
    squares, gates, ups = ([[] for _ in range(tp_size)] for _ in range(3))
    for (begin, columns), pieces, layout in zip(spans, x_refs, layouts):
        wide = jnp.concatenate(
            [pieces[p][at : at + block, :] for _, p, at in layout], axis=0
        ).astype(f32)
        square = None
        for j in range(0, columns, lanes):
            part = wide[:, j : j + lanes]
            square = part * part if square is None else square + part * part
        gain = gain_ref[:, begin : begin + columns].astype(f32)
        scaled = (wide * gain).astype(bf16)
        weights = jnp.concatenate(
            [gate_ref[begin : begin + columns, :], up_ref[begin : begin + columns, :]], axis=1
        )
        product = jnp.dot(scaled, weights, preferred_element_type=f32)
        gate, up = product[:, :hidden], product[:, hidden:]
        for i, (place, _, _) in enumerate(layout):
            rows = slice(i * block, (i + 1) * block)
            squares[place].append(square[rows])
            gates[place].append(gate[rows])
            ups[place].append(up[rows])

    for place in range(tp_size):
        rows = slice(place * block, (place + 1) * block)
        if last:
            squares[place].append(square_in[rows, :])
            gates[place].append(acc_in[rows, :hidden])
            ups[place].append(acc_in[rows, hidden:])
        elif not gates[place]:
            squares[place].append(jnp.zeros((block, lanes), f32))
            gates[place].append(jnp.zeros((block, hidden), f32))
            ups[place].append(jnp.zeros((block, hidden), f32))
        square, gate, up = (add(*found[place]) for found in (squares, gates, ups))
        if not last:
            square_ref[rows, :] = square
            acc_ref[rows, :hidden] = gate
            acc_ref[rows, hidden:] = up
            continue
        mean = jnp.sum(square, axis=-1, keepdims=True) * (1.0 / gate_ref.shape[0])
        scale = lax.rsqrt(mean + 1e-06)
        gate, up = gate * scale, up * scale
        active = gate / (1.0 + jnp.exp(-gate)) * up
        own = out_ref.shape[1] // tp_size
        at = pl.multiple_of(order_ref[place] * own, own)
        for m in range(out_ref.shape[0]):
            ordered[m, pl.ds(at, own), :] = active[m * own : (m + 1) * own]
    if last:
        out_ref[...] = ordered[...].astype(bf16)


def gated(order, pieces, spans, layouts, block, gain, gate, up, micro, carried):
    columns, hidden = gate.shape
    rows = tp_size * block
    last = carried is not None
    vmem = pl.BlockSpec(memory_space=pltpu.VMEM)
    args = [piece for stream in pieces for piece in stream] + [gain, gate, up]
    in_specs = [vmem] * len(args)
    if last:
        args = [order] + args + list(carried)
        in_specs = [pl.BlockSpec(memory_space=pltpu.SMEM)] + in_specs + [vmem] * 2
        out_dims = (micro, rows // micro, hidden)
        out_shape = jax.ShapeDtypeStruct(out_dims, bf16)
        out_specs, scratch = vmem, [pltpu.VMEM(out_dims, f32)]
    else:
        out_shape = [
            jax.ShapeDtypeStruct((rows, 2 * hidden), f32),
            jax.ShapeDtypeStruct((rows, 128), f32),
        ]
        out_specs, scratch = [vmem, vmem], []
    return pl.pallas_call(
        functools.partial(gated_kernel, spans, layouts, block, last),
        in_specs=in_specs,
        out_specs=out_specs,
        out_shape=out_shape,
        scratch_shapes=scratch,
        compiler_params=pltpu.CompilerParams(vmem_limit_bytes=vmem_limit),
        cost_estimate=pl.CostEstimate(
            flops=2 * rows * columns * hidden,
            bytes_accessed=4 * columns * hidden,
            transcendentals=0,
        ),
        name="gated_far" if last else "gated_near",
    )(*args)


def add(*parts):
    total = parts[0].astype(f32)
    for part in parts[1:]:
        total = total + part.astype(f32)
    return total


def shards(
    residual,
    queries,
    latent_cache,
    new_latent,
    lengths,
    positions,
    latent_value_weight,
    w_out,
    norm_gain,
    gate_weight,
    up_weight,
):
    latent = latent_value_weight.shape[1]
    micro, own_rows, width = residual.shape
    block = micro * own_rows
    heads = queries.shape[2]
    me = lax.axis_index("tp")
    places = [(c, p, q, z) for c in range(2) for p in range(2) for q in range(2) for z in range(2)]
    order = jnp.stack(
        [((me // 4) ^ p ^ (3 * q)) * 4 + (((me // 2) % 2) ^ z) * 2 + ((me % 2) ^ c) for c, p, q, z in places]
    ).astype(jnp.int32)
    attended = attention(
        queries.reshape((block,) + queries.shape[2:]),
        jnp.swapaxes(latent_cache, 2, 3).reshape(block, latent_cache.shape[3], -1),
        new_latent.reshape(block, -1),
        lengths,
        positions,
        latent,
    )
    arrived = lax.all_to_all(
        attended.reshape(tp_size, heads // tp_size, block, latent),
        "tp",
        split_axis=0,
        concat_axis=0,
        tiled=True,
    )

    streams = ("pqz", "qzp", "zpq")
    each = range(len(streams))
    step = -(-width // (len(streams) * 128)) * 128
    spans = [(i * step, min(step, width - i * step)) for i in each]
    names = "cpqz"
    orders, layouts = [], []
    for dims in streams:
        rank = [names.index(d) for d in "c" + dims]
        orders.append(sorted(range(tp_size), key=lambda i: [places[i][k] for k in rank]))
        layouts.append(
            [
                [
                    (i, at[rank[0]], (at[rank[2]] * 2 + at[rank[3]]) * block)
                    for i, at in enumerate(places)
                    if at[rank[1]] == side
                ]
                for side in range(2)
            ]
        )
    values = value_rows(order, arrived, latent_value_weight)
    projected = project(values, w_out, block, spans, orders)
    kept, sent = projected[0::2], projected[1::2]
    flat_residual = residual.reshape(block, width)

    pair = [add(kept[i], send(sent[i], "c")).astype(bf16) for i in each]
    four = [
        add(pair[i][: 4 * block], send(pair[i][4 * block :], streams[i][0])).astype(bf16)
        for i in each
    ]
    two = []
    for i in each:
        total = add(four[i][: 2 * block], send(four[i][2 * block :], streams[i][1]))
        begin, columns = spans[i]
        own = total[:block] + flat_residual[:, begin : begin + columns].astype(f32)
        two.append(jnp.concatenate([own, total[block:]], axis=0).astype(bf16))
    other = [send(two[i], streams[i][2]) for i in each]
    both = [
        jnp.concatenate(
            [add(two[i][:block], other[i][block:]), add(two[i][block:], other[i][:block])], axis=0
        ).astype(bf16)
        for i in each
    ]
    near = [jnp.concatenate([both[i], send(both[i], streams[i][1])], axis=0) for i in each]
    far = [send(near[i], streams[i][0]) for i in each]
    def products(sides, side, carried):
        return gated(
            order,
            [[sides[i], send(sides[i], "c")] for i in each],
            spans,
            [layout[side] for layout in layouts],
            block,
            norm_gain.reshape(1, width),
            gate_weight,
            up_weight,
            micro,
            carried,
        )

    carried = products(near, 0, None)
    for i in each:
        far[i], carried = lax.optimization_barrier((far[i], carried))
    activation = products(far, 1, carried)
    after_attention = jnp.concatenate([both[i][:block] for i in each], axis=1)
    return (after_attention.reshape(residual.shape), activation)


def solution(mesh):
    return jax.shard_map(
        shards,
        mesh=mesh,
        in_specs=(
            P(None, ("dp", "tp"), None),
            P(None, ("dp", "tp"), None, None),
            P(None, ("dp", "tp"), None, None),
            P(None, ("dp", "tp"), None),
            P(None, ("dp", "tp")),
            P(None, ("dp", "tp")),
            P("tp", None, None),
            P("tp", None),
            P(),
            P(None, "tp"),
            P(None, "tp"),
        ),
        out_specs=(P(None, ("dp", "tp"), None), P(None, "dp", "tp")),
        check_vma=False,
    )
```
